128 devices in a mesh: ctx: 8 (over y, core), tp: 16 (over x, z).
Axes of the slice: x: 4, y: 4, z: 4, core: 2. Of those that a mesh axis runs over, the one named last changes fastest.
Arguments:
- tokens: bfloat16 [16384, 2048], P('ctx', 'tp'), may hold values from -6 to 6
- cotangent: bfloat16 [16384, 2048], P('ctx', 'tp'), may hold values from -6 to 6
- w_query: bfloat16 [2048, 2048], P(None, 'tp'), may hold values from -0.243067956 to 0.243067956
- w_key: bfloat16 [2048, 2048], P(None, 'tp'), may hold values from -0.243067956 to 0.243067956
- w_value: bfloat16 [2048, 2048], P(None, 'tp'), may hold values from -0.125 to 0.125
- w_out: bfloat16 [2048, 2048], P('tp'), may hold values from -0.125 to 0.125
Outputs:
- token_grad: bfloat16 [16384, 2048], P('ctx', 'tp')
- query_grad: float32 [2048, 2048], P(None, 'tp')
- key_grad: float32 [2048, 2048], P(None, 'tp')
- value_grad: float32 [2048, 2048], P(None, 'tp')
- out_grad: float32 [2048, 2048], P('tp')
The draws below stay inside these ranges and needn't reach their ends.
All inputs are finite; a program needn't handle non-finite values.
Results may differ from the reference program's by a relative error of at most 0.017.
The reference program's roundings to bfloat16 on the way (of `probs_low`, `attended`, `d_attended`, `d_scores` and `d_queries`) count: a program that leaves them out, or rounds other values in their place, can miss the bound.
Values may be sent and summed in bfloat16 or wider, within the bound.
No kernel may reach another device: no remote copies, remote signals or barrier semaphores. Data moves between devices by JAX's collectives and lax.ppermute only.
A program may use at most 192 MiB of HBM per device.

```python
import math
import jax
import jax.numpy as jnp

D = 2048
H = 16
DH = 128
RATIO = 16
TOK_DEV = 2048
TOKENS = 16384
LEVELS = 3
N_CTX = 8


def shared_weights(key):
    return jnp.clip(jax.random.normal(key, (D, H * DH), jnp.float32), -6.0, 6.0)


def draw_tokens(key, part):
    key = jax.random.fold_in(key, 11)
    rough_key, amp_key, phase_key = jax.random.split(key, 3)
    amplitude = jnp.clip(jax.random.normal(amp_key, (4, D), jnp.float32), -2.5, 2.5)
    phases = jax.random.uniform(phase_key, (4, D), jnp.float32, -math.pi, math.pi)
    position = jnp.arange(TOKENS, dtype=jnp.float32)[:, None] / TOKENS
    smooth = jnp.zeros((TOKENS, D), jnp.float32)
    for f in range(4):
        smooth = smooth + amplitude[f][None, :] * jnp.cos(2.0 * math.pi * (f + 1) * position + phases[f][None, :])
    smooth = smooth * 0.5
    rough = jax.random.normal(rough_key, (TOKENS, D), jnp.float32)
    mixed = 0.8 * rough + 0.6 * smooth
    return jnp.clip(mixed, -6.0, 6.0).astype(jnp.bfloat16)


def draw_w_query(key, part):
    common = shared_weights(key)
    result = common * D ** (-0.5)
    return result.astype(jnp.bfloat16)


def draw_w_key(key, part):
    key = jax.random.fold_in(key, 22)
    own = jnp.clip(jax.random.normal(key, (D, H * DH), jnp.float32), -6.0, 6.0)
    result = own * D ** (-0.5)
    return result.astype(jnp.bfloat16)


def block_levels(own_key, shape, cuts, smallest, top_value):
    level, own = 1.0, jax.random.fold_in(own_key, 6)
    for dim, parts in cuts:
        steps = jnp.exp(jax.random.uniform(jax.random.fold_in(own, dim), (parts,), jnp.float32, smallest / len(cuts), top_value / len(cuts)))
        level = level * jnp.repeat(steps, shape[dim] // parts).reshape([-1 if axis == dim else 1 for axis in range(len(shape))])
    return level


def gaussian(rng, shape, scale, bound, cuts=(), held_as=jnp.bfloat16):
    values = jax.random.normal(rng, shape, jnp.float32) * scale
    if len(cuts) > 0:
        values = block_levels(rng, shape, cuts, -0.22, 0.18) * values
    return jnp.clip(values, min=-bound, max=bound).astype(held_as)


def setup_inputs(seed: int = 0) -> dict:
    key_list = jax.random.split(jax.random.key(seed), 7)
    return {
        "tokens": draw_tokens(jax.random.fold_in(key_list[6], 71), 0),
        "cotangent": gaussian(key_list[1], (TOKENS, D), 1.0, 6.0, ((0, 8), (1, 16))),
        "w_query": draw_w_query(jax.random.fold_in(key_list[6], 71), 0),
        "w_key": draw_w_key(jax.random.fold_in(key_list[6], 71), 0),
        "w_value": gaussian(key_list[4], (D, H * DH), D ** -0.5, 0.125, ((1, 16),)),
        "w_out": gaussian(key_list[5], (H * DH, D), (H * DH) ** -0.5, 0.125, ((0, 16),)),
    }


def pool_rows(values, width):
    return jnp.mean(values.astype(jnp.float32).reshape(values.shape[0] // width, width, values.shape[1]), axis=1).astype(jnp.bfloat16)


def reference(tokens, cotangent, w_query, w_key, w_value, w_out):
    score_scale = DH ** -0.5
    coarse = TOK_DEV // RATIO
    columns = H * DH
    queries = jnp.dot(tokens, w_query, preferred_element_type=jnp.float32).astype(jnp.bfloat16)
    key_rows = jnp.dot(tokens, w_key, preferred_element_type=jnp.float32).astype(jnp.bfloat16)
    value_rows = jnp.dot(tokens, w_value, preferred_element_type=jnp.float32).astype(jnp.bfloat16)
    pooled_keys = []
    pooled_values = []
    grad_keys = []
    grad_values = []
    for l in range(LEVELS):
        width = RATIO * 2 ** l
        pooled_keys.append(pool_rows(key_rows, width))
        pooled_values.append(pool_rows(value_rows, width))
        grad_keys.append(jnp.zeros((TOKENS // width, columns), jnp.float32))
        grad_values.append(jnp.zeros((TOKENS // width, columns), jnp.float32))
    attended_list = []
    dq_list = []
    dk_list = []
    dv_list = []
    for b in range(N_CTX):
        first = b * TOK_DEV
        key_parts = [key_rows[first:first + TOK_DEV]]
        value_parts = [value_rows[first:first + TOK_DEV]]
        bias_parts = [jnp.zeros((TOK_DEV,), jnp.float32)]
        row_starts = []
        for l in range(LEVELS):
            group = ((b >> l) ^ 1) << l
            row_first = group * (coarse >> l)
            row_starts.append(row_first)
            key_parts.append(pooled_keys[l][row_first:row_first + coarse])
            value_parts.append(pooled_values[l][row_first:row_first + coarse])
            bias_parts.append(jnp.full((coarse,), math.log(RATIO * 2 ** l), jnp.float32))
        keys_all = jnp.concatenate(key_parts, axis=0).astype(jnp.float32).reshape(-1, H, DH)
        values_all = jnp.concatenate(value_parts, axis=0).astype(jnp.float32).reshape(-1, H, DH)
        bias_all = jnp.concatenate(bias_parts)
        query_block = queries[first:first + TOK_DEV].astype(jnp.float32).reshape(TOK_DEV, H, DH)
        scores = jnp.einsum('thd,khd->htk', query_block, keys_all) * score_scale + bias_all[None, None, :]
        peak = jnp.max(scores, axis=-1, keepdims=True)
        expo = jnp.exp(scores - peak)
        probs = expo / jnp.sum(expo, axis=-1, keepdims=True)
        probs_low = probs.astype(jnp.bfloat16).astype(jnp.float32)
        attended = jnp.einsum('htk,khd->thd', probs_low, values_all).reshape(TOK_DEV, columns).astype(jnp.bfloat16)
        attended_list.append(attended)
        d_attended = jnp.dot(cotangent[first:first + TOK_DEV], w_out.T, preferred_element_type=jnp.float32).astype(jnp.bfloat16)
        d_attended4 = d_attended.astype(jnp.float32).reshape(TOK_DEV, H, DH)
        d_probs = jnp.einsum('thd,khd->htk', d_attended4, values_all)
        delta = jnp.sum(probs * d_probs, axis=-1, keepdims=True)
        d_scores = (score_scale * probs * (d_probs - delta)).astype(jnp.bfloat16).astype(jnp.float32)
        d_queries = jnp.einsum('htk,khd->thd', d_scores, keys_all).reshape(TOK_DEV, columns).astype(jnp.bfloat16)
        d_keys_all = jnp.einsum('htk,thd->khd', d_scores, query_block).reshape(-1, columns)
        d_values_all = jnp.einsum('htk,thd->khd', probs_low, d_attended4).reshape(-1, columns)
        dq_list.append(d_queries)
        dk_list.append(d_keys_all[:TOK_DEV])
        dv_list.append(d_values_all[:TOK_DEV])
        for l in range(LEVELS):
            low = TOK_DEV + l * coarse
            grad_keys[l] = grad_keys[l].at[row_starts[l]:row_starts[l] + coarse].add(d_keys_all[low:low + coarse])
            grad_values[l] = grad_values[l].at[row_starts[l]:row_starts[l] + coarse].add(d_values_all[low:low + coarse])
    key_total = jnp.concatenate(dk_list, axis=0)
    value_total = jnp.concatenate(dv_list, axis=0)
    for l in range(LEVELS):
        width = RATIO * 2 ** l
        key_total = key_total + jnp.repeat(grad_keys[l] / width, width, axis=0)
        value_total = value_total + jnp.repeat(grad_values[l] / width, width, axis=0)
    d_queries = jnp.concatenate(dq_list, axis=0)
    d_keys = key_total.astype(jnp.bfloat16)
    d_values = value_total.astype(jnp.bfloat16)
    attended = jnp.concatenate(attended_list, axis=0)
    token_grad = (jnp.dot(d_queries, w_query.T, preferred_element_type=jnp.float32)
                  + jnp.dot(d_keys, w_key.T, preferred_element_type=jnp.float32)
                  + jnp.dot(d_values, w_value.T, preferred_element_type=jnp.float32)).astype(jnp.bfloat16)
    query_grad = jnp.dot(tokens.T, d_queries, preferred_element_type=jnp.float32)
    key_grad = jnp.dot(tokens.T, d_keys, preferred_element_type=jnp.float32)
    value_grad = jnp.dot(tokens.T, d_values, preferred_element_type=jnp.float32)
    out_grad = jnp.dot(attended.T, cotangent, preferred_element_type=jnp.float32)
    return (token_grad, query_grad, key_grad, value_grad, out_grad)
```

```python
import functools
import math

import jax
import jax.numpy as jnp
from jax import lax
from jax.experimental import pallas as pl
from jax.experimental.pallas import tpu as pltpu
from jax.sharding import PartitionSpec as P

DH = 128
RATIO = 16
NX = 4
NZ = 4
NY = 4
BF = jnp.bfloat16
F32 = jnp.float32
STEPS = (0, 1, -1, 2)
LOG2E = 1.0 / math.log(2.0)
NT = (((1,), (1,)), ((), ()))
NN = (((1,), (0,)), ((), ()))


def mm(a, b, dims=NN):
    return lax.dot_general(a, b, dims, preferred_element_type=F32)


def place(ctx, first, second):
    x, z = (first, second) if ctx % 2 == 0 else (second, first)
    return ctx * NX * NZ + x * NZ + z


def send(value, first, second):
    pairs = [
        (place(ctx, a, b), place(ctx, (a + first) % NX, (b + second) % NZ))
        for ctx in range(NY * 2)
        for a in range(NX)
        for b in range(NZ)
    ]
    return lax.ppermute(value, ("ctx", "tp"), pairs)


def first_lines():
    return [
        [place(ctx, a, b) for a in range(NX)] for ctx in range(NY * 2) for b in range(NZ)
    ]


def position():
    me = lax.axis_index("tp")
    x, z = me // NZ, me % NZ
    even = lax.axis_index("ctx") % 2 == 0
    return even, jnp.where(even, x, z), jnp.where(even, z, x)


def send_core(value):
    return lax.ppermute(value, "ctx", [(i, i ^ 1) for i in range(NY * 2)])


def order_kernel(x_ref, dep_ref, out_ref):
    pass


def after(value, dep):
    return pl.pallas_call(
        order_kernel,
        in_specs=[pl.BlockSpec(memory_space=pl.ANY)] * 2,
        out_specs=pl.BlockSpec(memory_space=pl.ANY),
        out_shape=jax.ShapeDtypeStruct(value.shape, value.dtype),
        input_output_aliases={0: 0},
    )(value, dep)


def gather_features(block):
    up, down, far = [send(block, step, 0) for step in STEPS[1:]]
    near, rest = jnp.stack([block, up]), jnp.stack([down, far])
    near, rest = after(near, rest), after(rest, near)
    near_up, rest_down = send(near, 0, 1), send(rest, 0, -1)
    near_down, rest_up = send(near, 0, -1), send(rest, 0, 1)
    near_far, rest_far = send(near_up, 0, 1), send(rest_down, 0, -1)
    return [near, rest, near_up, rest_up, near_down, rest_down, near_far, rest_far]


def block_ids():
    even, first, second = position()
    ids = []
    for b in STEPS:
        for a in STEPS:
            i, j = (first - a) % NX, (second - b) % NZ
            ids.append(jnp.where(even, i * NZ + j, j * NZ + i))
    return jnp.stack(ids).astype(jnp.int32)


def project_kernel(ids, *refs):
    parts = refs[:8]
    w_ref, full_ref, q_ref, kv_ref = refs[8:12]
    pooled = refs[12:]
    for i in range(16):
        start = pl.multiple_of(ids[i] * 128, 128)
        full_ref[:, pl.ds(start, 128)] = parts[i // 2][i % 2]
    out = mm(full_ref[...], w_ref[...]).astype(BF)
    q_ref[...] = out[:, :DH]
    kv = out[:, DH:]
    kv_ref[...] = kv
    rows = kv.shape[0]
    for l, ref in enumerate(pooled):
        width = RATIO * 2**l
        window = lax.broadcasted_iota(jnp.int32, (rows // width, rows), 0)
        row = lax.broadcasted_iota(jnp.int32, (rows // width, rows), 1)
        inside = jnp.where((row >= window * width) & (row < (window + 1) * width), 1.0, 0.0)
        ref[...] = mm(inside.astype(BF), kv) * (1.0 / width)


def project(ids, parts, weight, levels):
    n = parts[0].shape[1]
    feats = 16 * 128
    rows = 512
    row_map = lambda i, ids: (i, 0)
    pooled = [n // (RATIO * 2**l) for l in range(levels)]
    return pl.pallas_call(
        project_kernel,
        grid_spec=pltpu.PrefetchScalarGridSpec(
            num_scalar_prefetch=1,
            grid=(n // rows,),
            in_specs=[pl.BlockSpec((2, rows, 128), lambda i, ids: (0, i, 0))] * 8
            + [pl.BlockSpec(weight.shape, lambda i, ids: (0, 0))],
            out_specs=[
                pl.BlockSpec((rows, feats), row_map),
                pl.BlockSpec((rows, DH), row_map),
                pl.BlockSpec((rows, 2 * DH), row_map),
            ]
            + [pl.BlockSpec((p * rows // n, 2 * DH), row_map) for p in pooled],
        ),
        out_shape=[
            jax.ShapeDtypeStruct((n, feats), BF),
            jax.ShapeDtypeStruct((n, DH), BF),
            jax.ShapeDtypeStruct((n, 2 * DH), BF),
        ]
        + [jax.ShapeDtypeStruct((p, 2 * DH), F32) for p in pooled],
        compiler_params=pltpu.CompilerParams(vmem_limit_bytes=60 * 2**20),
        cost_estimate=pl.CostEstimate(
            flops=6 * n * feats * DH, bytes_accessed=4 * n * feats, transcendentals=0
        ),
    )(ids, *parts, weight)


def add_bias(scores, own, coarse):
    out = [scores[:own]]
    for l in range((scores.shape[0] - own) // coarse):
        low = own + l * coarse
        out.append(scores[low : low + coarse] + math.log(RATIO * 2**l) * LOG2E)
    return jnp.concatenate(out, axis=0)


def forward_kernel(own, coarse, q_ref, kv_ref, sib_ref, att_ref, lse_ref, k_ref, vt_ref):
    @pl.when(pl.program_id(0) == 0)
    def _():
        k_ref[:own] = kv_ref[:, :DH]
        k_ref[own:] = sib_ref[:, :DH]
        vt_ref[:, :own] = kv_ref[:, DH:].T
        vt_ref[:, own:] = sib_ref[:, DH:].T

    scores = mm(k_ref[...], q_ref[...], NT) * (DH**-0.5 * LOG2E)
    scores = add_bias(scores, own, coarse)
    peak = jnp.max(scores, axis=0, keepdims=True)
    expo = jnp.exp2(scores - peak)
    total = jnp.sum(expo, axis=0, keepdims=True)
    probs = (expo * (1.0 / total)).astype(BF)
    att_ref[...] = mm(vt_ref[...], probs).astype(BF)
    lse_ref[...] = peak + jnp.log2(total)


def attend(queries, listed, siblings, coarse):
    n = queries.shape[0]
    own, more = listed.shape[0], siblings.shape[0]
    m = own + more
    rows = 256
    whole = lambda i: (0, 0)
    return pl.pallas_call(
        functools.partial(forward_kernel, own, coarse),
        grid=(n // rows,),
        in_specs=[
            pl.BlockSpec((rows, DH), lambda i: (i, 0)),
            pl.BlockSpec((own, 2 * DH), whole),
            pl.BlockSpec((more, 2 * DH), whole),
        ],
        out_specs=[
            pl.BlockSpec((DH, rows), lambda i: (0, i)),
            pl.BlockSpec((1, rows), lambda i: (0, i)),
        ],
        out_shape=[
            jax.ShapeDtypeStruct((DH, n), BF),
            jax.ShapeDtypeStruct((1, n), F32),
        ],
        scratch_shapes=[pltpu.VMEM((m, DH), BF), pltpu.VMEM((DH, m), BF)],
        compiler_params=pltpu.CompilerParams(vmem_limit_bytes=60 * 2**20),
        cost_estimate=pl.CostEstimate(
            flops=8 * n * m * DH, bytes_accessed=4 * n * DH, transcendentals=n * m
        ),
    )(queries, listed, siblings)


def backward_kernel(
    own, coarse, q_ref, kv_ref, sib_ref, cot_ref, wo_ref, lse_ref,
    dq_ref, dkv_ref, dsib_ref, k_ref, v_ref, kt_ref, acc_ref,
):
    step = pl.program_id(0)

    @pl.when(step == 0)
    def _():
        k_ref[:own] = kv_ref[:, :DH]
        k_ref[own:] = sib_ref[:, :DH]
        v_ref[:own] = kv_ref[:, DH:]
        v_ref[own:] = sib_ref[:, DH:]
        kt_ref[...] = k_ref[...].T
        acc_ref[...] = jnp.zeros_like(acc_ref)

    q = q_ref[...]
    da = mm(cot_ref[...], wo_ref[...], NT).astype(BF)
    scores = mm(k_ref[...], q, NT) * (DH**-0.5 * LOG2E)
    probs = jnp.exp2(add_bias(scores, own, coarse) - lse_ref[...])
    d_probs = mm(v_ref[...], da, NT)
    delta = jnp.sum(probs * d_probs, axis=0, keepdims=True)
    d_scores = (DH**-0.5 * probs * (d_probs - delta)).astype(BF)
    probs = probs.astype(BF)
    acc_ref[:, :DH] += mm(d_scores, q)
    acc_ref[:, DH:] += mm(probs, da)
    dq_ref[...] = mm(kt_ref[...], d_scores).T.astype(BF)

    @pl.when(step == pl.num_programs(0) - 1)
    def _():
        dkv_ref[...] = acc_ref[:own]
        dsib_ref[...] = acc_ref[own:]


def attend_back(queries, listed, siblings, cot, w_out, lse, coarse):
    n, feats = cot.shape
    own, more = listed.shape[0], siblings.shape[0]
    m = own + more
    rows = 256
    whole = lambda i: (0, 0)
    return pl.pallas_call(
        functools.partial(backward_kernel, own, coarse),
        grid=(n // rows,),
        in_specs=[
            pl.BlockSpec((rows, DH), lambda i: (i, 0)),
            pl.BlockSpec((own, 2 * DH), whole),
            pl.BlockSpec((more, 2 * DH), whole),
            pl.BlockSpec((rows, feats), lambda i: (i, 0)),
            pl.BlockSpec((DH, feats), whole),
            pl.BlockSpec((1, rows), lambda i: (0, i)),
        ],
        out_specs=[
            pl.BlockSpec((rows, DH), lambda i: (i, 0)),
            pl.BlockSpec((own, 2 * DH), whole),
            pl.BlockSpec((more, 2 * DH), whole),
        ],
        out_shape=[
            jax.ShapeDtypeStruct((n, DH), BF),
            jax.ShapeDtypeStruct((own, 2 * DH), F32),
            jax.ShapeDtypeStruct((more, 2 * DH), F32),
        ],
        scratch_shapes=[
            pltpu.VMEM((m, DH), BF),
            pltpu.VMEM((m, DH), BF),
            pltpu.VMEM((DH, m), BF),
            pltpu.VMEM((m, 2 * DH), F32),
        ],
        compiler_params=pltpu.CompilerParams(vmem_limit_bytes=60 * 2**20),
        cost_estimate=pl.CostEstimate(
            flops=20 * n * m * DH, bytes_accessed=2 * n * feats, transcendentals=n * m
        ),
    )(queries, listed, siblings, cot, w_out, lse)


def token_grad_kernel(ids, d_ref, *refs):
    weights, outs = refs[:NZ], refs[NZ:]
    d = jnp.concatenate([d_ref[i] for i in range(NX)], axis=1)
    w = jnp.concatenate([w[...].reshape(d.shape[1], DH) for w in weights], axis=1)
    out = mm(d, w)
    for step in range(NZ):
        outs[step][0] = out[:, step * DH : (step + 1) * DH]


def token_grad_parts(d_rows, weights):
    heads, rows, cols = d_rows.shape
    even, _, second = position()
    ids = []
    for i in range(NX):
        for step in range(NZ):
            j = (second + step) % NZ
            ids.append(jnp.where(even, i * NZ + j, j * NZ + i))
    ids = jnp.stack(ids).astype(jnp.int32)

    def column(step):
        return pl.BlockSpec((heads, cols, DH), lambda i, ids: (0, 0, ids[i * NZ + step]))

    return pl.pallas_call(
        token_grad_kernel,
        grid_spec=pltpu.PrefetchScalarGridSpec(
            num_scalar_prefetch=1,
            grid=(NX,),
            in_specs=[pl.BlockSpec((heads, rows, cols), lambda i, ids: (0, 0, 0))]
            + [column(step) for step in range(NZ)],
            out_specs=[pl.BlockSpec((1, rows, DH), lambda i, ids: (i, 0, 0))] * NZ,
        ),
        out_shape=[jax.ShapeDtypeStruct((NX, rows, DH), F32)] * NZ,
        compiler_params=pltpu.CompilerParams(vmem_limit_bytes=60 * 2**20),
        cost_estimate=pl.CostEstimate(
            flops=2 * heads * rows * cols * 2048,
            bytes_accessed=2 * heads * cols * 2048 + 8192 * rows,
            transcendentals=0,
        ),
    )(ids, d_rows, weights, weights, weights, weights)


def weight_grad_kernel(x_ref, d_ref, *refs):
    outs, dt_ref = refs[:-1], refs[-1]

    @pl.when(pl.program_id(0) == 0)
    def _():
        dt_ref[...] = d_ref[...].T

    grads = mm(dt_ref[...], x_ref[...]).T
    for i, out_ref in enumerate(outs):
        out_ref[...] = grads[:, i * DH : (i + 1) * DH]


def weight_grads(feats, grads):
    n, f = feats.shape
    count = grads.shape[1] // DH
    cols = 512
    return pl.pallas_call(
        weight_grad_kernel,
        grid=(f // cols,),
        in_specs=[
            pl.BlockSpec((n, cols), lambda i: (0, i)),
            pl.BlockSpec(grads.shape, lambda i: (0, 0)),
        ],
        out_specs=[pl.BlockSpec((cols, DH), lambda i: (i, 0))] * count,
        out_shape=[jax.ShapeDtypeStruct((f, DH), F32)] * count,
        scratch_shapes=[pltpu.VMEM((count * DH, n), BF)],
        compiler_params=pltpu.CompilerParams(vmem_limit_bytes=60 * 2**20),
        cost_estimate=pl.CostEstimate(
            flops=2 * n * f * DH * count,
            bytes_accessed=2 * n * f + 4 * f * DH * count,
            transcendentals=0,
        ),
    )(feats, grads)


def sibling_rows():
    me = lax.axis_index("ctx")
    return ((me >> 1) ^ 1) * 2, ((me >> 2) ^ 1) * 4


def fetch_pooled(pooled):
    half = pooled[1].shape[0]
    me = lax.axis_index("ctx")
    third = jnp.concatenate([pooled[2], pooled[2]], axis=0)
    buffer = jnp.stack([jnp.where((me ^ d) >= 4, third, pooled[1]) for d in range(NY * 2)])
    got = lax.all_to_all(buffer, "ctx", 0, 0)
    second, last = sibling_rows()
    cols = buffer.shape[2]
    level1 = lax.dynamic_slice_in_dim(got, second, 2, 0).reshape(2 * half, cols)
    level2 = lax.dynamic_slice_in_dim(got, last, 4, 0)[:, : half // 2].reshape(2 * half, cols)
    return [send_core(pooled[0]), level1, level2]


def return_pooled(grads, coarse, *meanwhile):
    half, cols = coarse // 2, grads.shape[1]
    second, last = sibling_rows()
    level1 = grads[coarse : 2 * coarse].reshape(2, half, cols)
    level2 = grads[2 * coarse :].reshape(4, half // 2, cols)
    level2 = jnp.concatenate([level2, jnp.zeros_like(level2)], axis=1)
    buffer = jnp.zeros((NY * 2, half, cols), F32)
    buffer = lax.dynamic_update_slice_in_dim(buffer, level1, second, 0)
    buffer = lax.dynamic_update_slice_in_dim(buffer, level2, last, 0)
    got = lax.all_to_all(buffer, "ctx", 0, 0)
    for done in meanwhile:
        got = after(got, done)
    level1 = jnp.sum(lax.dynamic_slice_in_dim(got, second, 2, 0), axis=0)
    level2 = jnp.sum(lax.dynamic_slice_in_dim(got, last, 4, 0)[:, : half // 2], axis=0)
    return [send_core(grads[:coarse]), level1, level2]


def body(tokens, cotangent, w_query, w_key, w_value, w_out):
    own = tokens.shape[0]
    coarse = own // RATIO
    levels = 3
    ids = block_ids()
    weights = jnp.concatenate([w_query, w_key, w_value], axis=1)
    tok_parts = gather_features(tokens)
    cot = lax.all_gather(after(cotangent, tok_parts[1]), "tp", axis=1, tiled=True)
    feats, queries, keys_values, *pooled = project(ids, tok_parts, weights, levels)
    pooled = [p.astype(BF) for p in pooled]
    siblings = jnp.concatenate(fetch_pooled(pooled), axis=0)
    attended_t, lse = attend(queries, keys_values, siblings, coarse)
    lines = first_lines()
    weight_heads = lax.all_gather(
        after(weights.T, queries), ("ctx", "tp"), axis_index_groups=lines
    )

    out_part = mm(attended_t, cot)
    d_queries, total, d_siblings = attend_back(
        queries, keys_values, siblings, cot, w_out, lse, coarse
    )
    grads = return_pooled(d_siblings, coarse, out_part)
    for l in range(levels):
        width = RATIO * 2**l
        total = total + jnp.broadcast_to(
            grads[l][:, None, :] / width, (own // width, width, 2 * DH)
        ).reshape(own, 2 * DH)
    d_all = jnp.concatenate([d_queries, total.astype(BF)], axis=1)
    query_grad, key_grad, value_grad, out_grad = lax.psum(
        tuple(weight_grads(feats, d_all)) + (out_part,), "ctx"
    )
    d_rows = d_all.reshape(NX, own // NX, 3 * DH)
    d_rows = lax.all_to_all(d_rows, ("ctx", "tp"), 0, 0, axis_index_groups=lines)
    parts = token_grad_parts(d_rows, weight_heads)
    total = parts[0]
    for step in range(1, NZ):
        total = total + send(parts[step], 0, step)
    token_grad = lax.all_to_all(
        total.astype(BF), ("ctx", "tp"), 0, 0, axis_index_groups=lines
    ).reshape(own, DH)
    return (token_grad, query_grad, key_grad, value_grad, out_grad)


def solution(mesh):
    return jax.shard_map(
        body,
        mesh=mesh,
        in_specs=(
            P("ctx", "tp"),
            P("ctx", "tp"),
            P(None, "tp"),
            P(None, "tp"),
            P(None, "tp"),
            P("tp", None),
        ),
        out_specs=(P("ctx", "tp"), P(None, "tp"), P(None, "tp"), P(None, "tp"), P("tp", None)),
        check_vma=False,
    )
```

```python
import functools
import math

import jax
import jax.numpy as jnp
from jax import lax
from jax.experimental import pallas as pl
from jax.experimental.pallas import tpu as pltpu
from jax.sharding import PartitionSpec as P

DH = 128
RATIO = 16
NX = 4
NZ = 4
NY = 4
BF = jnp.bfloat16
F32 = jnp.float32
STEPS = (0, 1, -1, 2)
LOG2E = 1.0 / math.log(2.0)
NT = (((1,), (1,)), ((), ()))
NN = (((1,), (0,)), ((), ()))


def mm(a, b, dims=NN):
    return lax.dot_general(a, b, dims, preferred_element_type=F32)


def place(ctx, first, second):
    x, z = (first, second) if ctx % 2 == 0 else (second, first)
    return ctx * NX * NZ + x * NZ + z


def send(value, first, second):
    pairs = [
        (place(ctx, a, b), place(ctx, (a + first) % NX, (b + second) % NZ))
        for ctx in range(NY * 2)
        for a in range(NX)
        for b in range(NZ)
    ]
    return lax.ppermute(value, ("ctx", "tp"), pairs)


def first_lines():
    return [
        [place(ctx, a, b) for a in range(NX)] for ctx in range(NY * 2) for b in range(NZ)
    ]


def position():
    me = lax.axis_index("tp")
    x, z = me // NZ, me % NZ
    even = lax.axis_index("ctx") % 2 == 0
    return even, jnp.where(even, x, z), jnp.where(even, z, x)


def send_core(value):
    return lax.ppermute(value, "ctx", [(i, i ^ 1) for i in range(NY * 2)])


def order_kernel(x_ref, dep_ref, out_ref):
    pass


def after(value, dep):
    return pl.pallas_call(
        order_kernel,
        in_specs=[pl.BlockSpec(memory_space=pl.ANY)] * 2,
        out_specs=pl.BlockSpec(memory_space=pl.ANY),
        out_shape=jax.ShapeDtypeStruct(value.shape, value.dtype),
        input_output_aliases={0: 0},
    )(value, dep)


def gather_features(block):
    up, down, far = [send(block, step, 0) for step in STEPS[1:]]
    near, rest = jnp.stack([block, up]), jnp.stack([down, far])
    near, rest = after(near, rest), after(rest, near)
    near_up, rest_down = send(near, 0, 1), send(rest, 0, -1)
    near_down, rest_up = send(near, 0, -1), send(rest, 0, 1)
    near_far, rest_far = send(near_up, 0, 1), send(rest_down, 0, -1)
    return [near, rest, near_up, rest_up, near_down, rest_down, near_far, rest_far]


def block_ids():
    even, first, second = position()
    ids = []
    for b in STEPS:
        for a in STEPS:
            i, j = (first - a) % NX, (second - b) % NZ
            ids.append(jnp.where(even, i * NZ + j, j * NZ + i))
    return jnp.stack(ids).astype(jnp.int32)


def sibling_ids():
    me = lax.axis_index("ctx")
    return jnp.stack([((me >> 1) ^ 1) * 2, ((me >> 2) ^ 1) * 4]).astype(jnp.int32)


def project_kernel(ids, sibs, *refs):
    parts = refs[:8]
    w_ref, full_ref, q_ref, kv_ref, first_ref, others_ref, second_ref, last_ref = refs[8:]
    step = pl.program_id(0)
    for i in range(16):
        start = pl.multiple_of(ids[i] * 128, 128)
        full_ref[:, pl.ds(start, 128)] = parts[i // 2][i % 2]
    out = mm(full_ref[...], w_ref[...]).astype(BF)
    q_ref[...] = out[:, :DH]
    kv = out[:, DH:]
    kv_ref[...] = kv
    rows = kv.shape[0]
    for l, ref in enumerate((first_ref, second_ref, last_ref)):
        width = RATIO * 2**l
        count = rows // width
        window = lax.broadcasted_iota(jnp.int32, (count, rows), 0)
        row = lax.broadcasted_iota(jnp.int32, (count, rows), 1)
        inside = jnp.where((row >= window * width) & (row < (window + 1) * width), 1.0, 0.0)
        means = mm(inside.astype(BF), kv) * (1.0 / width)
        if l == 0:
            ref[...] = means.astype(BF)
        else:
            ref[pl.ds(pl.multiple_of(step * count, count), count), :] = means

    @pl.when(step == pl.num_programs(0) - 1)
    def _():
        second = second_ref[...].astype(BF)
        last = last_ref[...].astype(BF)
        for d in range(NY * 2):
            others_ref[d] = second
        for d in range(4):
            others_ref[pl.ds(sibs[1] + d, 1), : last.shape[0]] = last[None]


def project(ids, sibs, parts, weight):
    n = parts[0].shape[1]
    feats = 16 * 128
    rows = 512
    row_map = lambda i, ids, sibs: (i, 0)
    coarse = n // RATIO
    return pl.pallas_call(
        project_kernel,
        grid_spec=pltpu.PrefetchScalarGridSpec(
            num_scalar_prefetch=2,
            grid=(n // rows,),
            in_specs=[pl.BlockSpec((2, rows, 128), lambda i, ids, sibs: (0, i, 0))] * 8
            + [pl.BlockSpec(weight.shape, lambda i, ids, sibs: (0, 0))],
            out_specs=[
                pl.BlockSpec((rows, feats), row_map),
                pl.BlockSpec((rows, DH), row_map),
                pl.BlockSpec((rows, 2 * DH), row_map),
                pl.BlockSpec((rows // RATIO, 2 * DH), row_map),
                pl.BlockSpec((NY * 2, coarse // 2, 2 * DH), lambda i, ids, sibs: (0, 0, 0)),
            ],
            scratch_shapes=[
                pltpu.VMEM((coarse // 2, 2 * DH), F32),
                pltpu.VMEM((coarse // 4, 2 * DH), F32),
            ],
        ),
        out_shape=[
            jax.ShapeDtypeStruct((n, feats), BF),
            jax.ShapeDtypeStruct((n, DH), BF),
            jax.ShapeDtypeStruct((n, 2 * DH), BF),
            jax.ShapeDtypeStruct((coarse, 2 * DH), BF),
            jax.ShapeDtypeStruct((NY * 2, coarse // 2, 2 * DH), BF),
        ],
        compiler_params=pltpu.CompilerParams(vmem_limit_bytes=60 * 2**20),
        cost_estimate=pl.CostEstimate(
            flops=6 * n * feats * DH, bytes_accessed=4 * n * feats, transcendentals=0
        ),
    )(ids, sibs, *parts, weight)


def add_bias(scores, own, coarse):
    out = [scores[:own]]
    for l in range((scores.shape[0] - own) // coarse):
        low = own + l * coarse
        out.append(scores[low : low + coarse] + math.log(RATIO * 2**l) * LOG2E)
    return jnp.concatenate(out, axis=0)


def attention_kernel(
    own, coarse, sibs, q_ref, kv_ref, first_ref, others_ref, cot_ref, wo_ref,
    att_ref, dq_ref, dkv_ref, dfirst_ref, dothers_ref, k_ref, v_ref, kt_ref, vt_ref, acc_ref,
):
    step = pl.program_id(0)

    @pl.when(step == 0)
    def _():
        half, quarter = coarse // 2, coarse // 4
        pieces = [(0, kv_ref[...]), (own, first_ref[...])]
        for d in range(2):
            pieces.append((own + coarse + d * half, others_ref[pl.ds(sibs[0] + d, 1)][0]))
        for d in range(4):
            rows = others_ref[pl.ds(sibs[1] + d, 1)][0, :quarter]
            pieces.append((own + 2 * coarse + d * quarter, rows))
        for low, rows in pieces:
            k_ref[low : low + rows.shape[0]] = rows[:, :DH]
            v_ref[low : low + rows.shape[0]] = rows[:, DH:]
        kt_ref[...] = k_ref[...].T
        vt_ref[...] = v_ref[...].T
        acc_ref[...] = jnp.zeros_like(acc_ref)

    q = q_ref[...]
    d_att = mm(cot_ref[...], wo_ref[...], NT).astype(BF)
    scores = mm(k_ref[...], q, NT) * (DH**-0.5 * LOG2E)
    scores = add_bias(scores, own, coarse)
    d_probs = mm(v_ref[...], d_att, NT)
    peak = jnp.max(scores, axis=0, keepdims=True)
    expo = jnp.exp2(scores - peak)
    probs = expo * (1.0 / jnp.sum(expo, axis=0, keepdims=True))
    delta = jnp.sum(probs * d_probs, axis=0, keepdims=True)
    d_scores = (DH**-0.5 * probs * (d_probs - delta)).astype(BF)
    probs = probs.astype(BF)
    att_ref[...] = mm(vt_ref[...], probs).astype(BF)
    dq_ref[...] = mm(kt_ref[...], d_scores).T.astype(BF)
    acc_ref[:, :DH] += mm(d_scores, q)
    acc_ref[:, DH:] += mm(probs, d_att)

    @pl.when(step == pl.num_programs(0) - 1)
    def _():
        half, quarter = coarse // 2, coarse // 4
        dkv_ref[...] = acc_ref[:own]
        dfirst_ref[...] = acc_ref[own : own + coarse]
        dothers_ref[...] = jnp.zeros_like(dothers_ref)
        for d in range(2):
            low = own + coarse + d * half
            dothers_ref[pl.ds(sibs[0] + d, 1)] = acc_ref[low : low + half][None]
        for d in range(4):
            low = own + 2 * coarse + d * quarter
            dothers_ref[pl.ds(sibs[1] + d, 1), :quarter] = acc_ref[low : low + quarter][None]


def attention(sibs, queries, listed, first, others, cot, w_out):
    n, feats = cot.shape
    own, coarse = listed.shape[0], first.shape[0]
    m = own + 3 * coarse
    rows = 512
    whole = lambda i, sibs: (0, 0)
    blocks = lambda i, sibs: (0, 0, 0)
    return pl.pallas_call(
        functools.partial(attention_kernel, own, coarse),
        grid_spec=pltpu.PrefetchScalarGridSpec(
            num_scalar_prefetch=1,
            grid=(n // rows,),
            in_specs=[
                pl.BlockSpec((rows, DH), lambda i, sibs: (i, 0)),
                pl.BlockSpec(listed.shape, whole),
                pl.BlockSpec(first.shape, whole),
                pl.BlockSpec(others.shape, blocks),
                pl.BlockSpec((rows, feats), lambda i, sibs: (i, 0)),
                pl.BlockSpec((DH, feats), whole),
            ],
            out_specs=[
                pl.BlockSpec((DH, rows), lambda i, sibs: (0, i)),
                pl.BlockSpec((rows, DH), lambda i, sibs: (i, 0)),
                pl.BlockSpec(listed.shape, whole),
                pl.BlockSpec(first.shape, whole),
                pl.BlockSpec(others.shape, blocks),
            ],
            scratch_shapes=[
                pltpu.VMEM((m, DH), BF),
                pltpu.VMEM((m, DH), BF),
                pltpu.VMEM((DH, m), BF),
                pltpu.VMEM((DH, m), BF),
                pltpu.VMEM((m, 2 * DH), F32),
            ],
        ),
        out_shape=[
            jax.ShapeDtypeStruct((DH, n), BF),
            jax.ShapeDtypeStruct((n, DH), BF),
            jax.ShapeDtypeStruct(listed.shape, F32),
            jax.ShapeDtypeStruct(first.shape, F32),
            jax.ShapeDtypeStruct(others.shape, F32),
        ],
        compiler_params=pltpu.CompilerParams(vmem_limit_bytes=60 * 2**20),
        cost_estimate=pl.CostEstimate(
            flops=24 * n * m * DH, bytes_accessed=2 * n * feats, transcendentals=n * m
        ),
    )(sibs, queries, listed, first, others, cot, w_out)


def token_grad_kernel(ids, d_ref, *refs):
    weights, outs = refs[:NZ], refs[NZ:]
    d = jnp.concatenate([d_ref[i] for i in range(NX)], axis=1)
    w = jnp.concatenate(
        [jnp.concatenate([w_ref[i] for w_ref in weights], axis=0) for i in range(NX)], axis=1
    )
    out = mm(d, w, NT)
    for step, out_ref in enumerate(outs):
        out_ref[0] = out[:, step * DH : (step + 1) * DH]


def token_grad_parts(d_rows, weights):
    heads, rows, cols = d_rows.shape
    even, _, second = position()
    ids = []
    for i in range(NX):
        for step in range(NZ):
            j = (second + step) % NZ
            ids.append(jnp.where(even, i * NZ + j, j * NZ + i))
    ids = jnp.stack(ids).astype(jnp.int32)

    def column(step):
        return pl.BlockSpec((heads, DH, cols), lambda i, ids: (0, ids[i * NZ + step], 0))

    return pl.pallas_call(
        token_grad_kernel,
        grid_spec=pltpu.PrefetchScalarGridSpec(
            num_scalar_prefetch=1,
            grid=(NX,),
            in_specs=[pl.BlockSpec((heads, rows, cols), lambda i, ids: (0, 0, 0))]
            + [column(step) for step in range(NZ)],
            out_specs=[pl.BlockSpec((1, rows, DH), lambda i, ids: (i, 0, 0))] * NZ,
        ),
        out_shape=[jax.ShapeDtypeStruct((NX, rows, DH), F32)] * NZ,
        compiler_params=pltpu.CompilerParams(vmem_limit_bytes=60 * 2**20),
        cost_estimate=pl.CostEstimate(
            flops=2 * heads * rows * cols * 2048,
            bytes_accessed=2 * heads * cols * 2048 + 8192 * rows,
            transcendentals=0,
        ),
    )(ids, d_rows, weights, weights, weights, weights)


def chunk_ids():
    c = lax.axis_index("ctx") % 2
    return jnp.stack([j * 2 + core for core in (1 - c, c) for j in range(NY)]).astype(jnp.int32)


def out_grad_kernel(chunks, x_ref, a_ref, give_ref, keep_ref):
    step = pl.program_id(0)
    grads = mm(a_ref[...], x_ref[...]).T

    @pl.when(step < NY)
    def _():
        give_ref[0, 0] = grads

    @pl.when(step >= NY)
    def _():
        keep_ref[0, 0] = grads


def out_grads(chunks, cot, attended_t):
    n, f = cot.shape
    cols = f // (2 * NY)
    shape = jax.ShapeDtypeStruct((NY, 4, cols, DH), F32)
    return pl.pallas_call(
        out_grad_kernel,
        grid_spec=pltpu.PrefetchScalarGridSpec(
            num_scalar_prefetch=1,
            grid=(2 * NY,),
            in_specs=[
                pl.BlockSpec((n, cols), lambda i, chunks: (0, chunks[i])),
                pl.BlockSpec((DH, n), lambda i, chunks: (0, 0)),
            ],
            out_specs=[
                pl.BlockSpec(
                    (1, 1, cols, DH), lambda i, chunks: (jnp.minimum(i, NY - 1), 3, 0, 0)
                ),
                pl.BlockSpec(
                    (1, 1, cols, DH), lambda i, chunks: (jnp.maximum(i - NY, 0), 3, 0, 0)
                ),
            ],
        ),
        out_shape=[shape, shape],
        compiler_params=pltpu.CompilerParams(vmem_limit_bytes=60 * 2**20),
        cost_estimate=pl.CostEstimate(
            flops=2 * n * f * DH, bytes_accessed=2 * n * f, transcendentals=0
        ),
    )(chunks, cot, attended_t)


def store_grads(out_ref, d_t, x):
    grads = mm(d_t, x).T
    for i in range(3):
        out_ref[0, i] = grads[:, i * DH : (i + 1) * DH]


def give_kernel(
    chunks, sibs, x_ref, dq_ref, own_ref, first_ref, others_ref, alias_ref, out_ref, d_ref, dt_ref
):
    @pl.when(pl.program_id(0) == 0)
    def _():
        coarse, cols = first_ref.shape
        half, quarter = coarse // 2, coarse // 4
        second = sum(others_ref[pl.ds(sibs[0] + d, 1)][0] for d in range(2))
        last = sum(others_ref[pl.ds(sibs[1] + d, 1)][0, :quarter] for d in range(4))
        total = own_ref[...]
        for l, grads in enumerate((first_ref[...], second, last)):
            width = RATIO * 2**l
            spread = jnp.broadcast_to(
                (grads * (1.0 / width))[:, None, :], (grads.shape[0], width, cols)
            )
            total = total + spread.reshape(total.shape)
        d_ref[:, :DH] = dq_ref[...]
        d_ref[:, DH:] = total.astype(BF)
        dt_ref[...] = d_ref[...].T

    store_grads(out_ref, dt_ref[...], x_ref[...])


def keep_kernel(chunks, x_ref, dt_ref, alias_ref, out_ref):
    store_grads(out_ref, dt_ref[...], x_ref[...])


def weight_grads_give(chunks, sibs, feats, d_queries, own, first, others, give):
    n, f = feats.shape
    cols = f // (2 * NY)
    whole = lambda i, chunks, sibs: (0, 0)
    return pl.pallas_call(
        give_kernel,
        grid_spec=pltpu.PrefetchScalarGridSpec(
            num_scalar_prefetch=2,
            grid=(NY,),
            in_specs=[
                pl.BlockSpec((n, cols), lambda i, chunks, sibs: (0, chunks[i])),
                pl.BlockSpec(d_queries.shape, whole),
                pl.BlockSpec(own.shape, whole),
                pl.BlockSpec(first.shape, whole),
                pl.BlockSpec(others.shape, lambda i, chunks, sibs: (0, 0, 0)),
                pl.BlockSpec(memory_space=pl.ANY),
            ],
            out_specs=[
                pl.BlockSpec((1, 3, cols, DH), lambda i, chunks, sibs: (i, 0, 0, 0)),
                pl.BlockSpec((n, 3 * DH), whole),
                pl.BlockSpec((3 * DH, n), whole),
            ],
        ),
        out_shape=[
            jax.ShapeDtypeStruct(give.shape, F32),
            jax.ShapeDtypeStruct((n, 3 * DH), BF),
            jax.ShapeDtypeStruct((3 * DH, n), BF),
        ],
        input_output_aliases={7: 0},
        compiler_params=pltpu.CompilerParams(vmem_limit_bytes=60 * 2**20),
        cost_estimate=pl.CostEstimate(
            flops=3 * n * f * DH, bytes_accessed=n * f + 6 * f * DH, transcendentals=0
        ),
    )(chunks, sibs, feats, d_queries, own, first, others, give)


def weight_grads_keep(chunks, feats, d_t, keep):
    n, f = feats.shape
    cols = f // (2 * NY)
    return pl.pallas_call(
        keep_kernel,
        grid_spec=pltpu.PrefetchScalarGridSpec(
            num_scalar_prefetch=1,
            grid=(NY,),
            in_specs=[
                pl.BlockSpec((n, cols), lambda i, chunks: (0, chunks[NY + i])),
                pl.BlockSpec(d_t.shape, lambda i, chunks: (0, 0)),
                pl.BlockSpec(memory_space=pl.ANY),
            ],
            out_specs=pl.BlockSpec((1, 3, cols, DH), lambda i, chunks: (i, 0, 0, 0)),
        ),
        out_shape=jax.ShapeDtypeStruct(keep.shape, F32),
        input_output_aliases={3: 0},
        compiler_params=pltpu.CompilerParams(vmem_limit_bytes=60 * 2**20),
        cost_estimate=pl.CostEstimate(
            flops=3 * n * f * DH, bytes_accessed=n * f + 6 * f * DH, transcendentals=0
        ),
    )(chunks, feats, d_t, keep)


def sum_ctx(give, keep, dep):
    halves = keep + send_core(give)
    columns = [[y * 2 + c for y in range(NY)] for c in range(2)]
    total = lax.psum_scatter(halves, "ctx", scatter_dimension=0, axis_index_groups=columns)
    grads = lax.all_gather(after(total, dep), "ctx")
    rows = grads.shape[0] * grads.shape[2]
    return [grads[:, i].reshape(rows, DH) for i in range(4)]


def body(tokens, cotangent, w_query, w_key, w_value, w_out):
    own = tokens.shape[0]
    ids, sibs, lines = block_ids(), sibling_ids(), first_lines()
    weights = jnp.concatenate([w_query, w_key, w_value], axis=1)
    tok_parts = gather_features(tokens)
    cot = lax.all_gather(after(cotangent, tok_parts[1]), "tp", axis=1, tiled=True)
    feats, queries, keys_values, first, others = project(ids, sibs, tok_parts, weights)
    others = lax.all_to_all(others, "ctx", 0, 0)
    first = send_core(first)
    weight_heads = lax.all_gather(
        after(weights, queries), ("ctx", "tp"), axis_index_groups=lines
    )
    attended_t, d_queries, d_own, d_first, d_others = attention(
        sibs, queries, keys_values, first, others, cot, w_out
    )
    chunks = chunk_ids()
    give, keep = out_grads(chunks, cot, attended_t)
    d_others = lax.all_to_all(d_others, "ctx", 0, 0)
    d_first = send_core(d_first)
    give, d_all, d_t = weight_grads_give(
        chunks, sibs, feats, d_queries, d_own, d_first, d_others, give
    )
    keep = weight_grads_keep(chunks, feats, d_t, keep)
    d_rows = d_all.reshape(NX, own // NX, 3 * DH)
    d_rows = lax.all_to_all(d_rows, ("ctx", "tp"), 0, 0, axis_index_groups=lines)
    parts = token_grad_parts(d_rows, weight_heads)
    query_grad, key_grad, value_grad, out_grad = sum_ctx(give, keep, parts[0])
    out_grad = out_grad.T
    total = parts[0]
    for step in range(1, NZ):
        total = total + send(parts[step], 0, step)
    token_grad = lax.all_to_all(
        total.astype(BF), ("ctx", "tp"), 0, 0, axis_index_groups=lines
    ).reshape(own, DH)
    return (token_grad, query_grad, key_grad, value_grad, out_grad)


def solution(mesh):
    return jax.shard_map(
        body,
        mesh=mesh,
        in_specs=(
            P("ctx", "tp"),
            P("ctx", "tp"),
            P(None, "tp"),
            P(None, "tp"),
            P(None, "tp"),
            P("tp", None),
        ),
        out_specs=(P("ctx", "tp"), P(None, "tp"), P(None, "tp"), P(None, "tp"), P("tp", None)),
        check_vma=False,
    )
```

```python
import functools
import math

import jax
import jax.numpy as jnp
from jax import lax
from jax.experimental import pallas as pl
from jax.experimental.pallas import tpu as pltpu
from jax.sharding import PartitionSpec as P

DH = 128
RATIO = 16
NX = 4
NZ = 4
NY = 4
BF = jnp.bfloat16
F32 = jnp.float32
STEPS = (0, 1, -1, 2)
LOG2E = 1.0 / math.log(2.0)
NT = (((1,), (1,)), ((), ()))
NN = (((1,), (0,)), ((), ()))


def mm(a, b, dims=NN):
    return lax.dot_general(a, b, dims, preferred_element_type=F32)


def place(ctx, first, second):
    x, z = (first, second) if ctx % 2 == 0 else (second, first)
    return ctx * NX * NZ + x * NZ + z


def send(value, first, second):
    pairs = [
        (place(ctx, a, b), place(ctx, (a + first) % NX, (b + second) % NZ))
        for ctx in range(NY * 2)
        for a in range(NX)
        for b in range(NZ)
    ]
    return lax.ppermute(value, ("ctx", "tp"), pairs)


def first_lines():
    return [
        [place(ctx, a, b) for a in range(NX)] for ctx in range(NY * 2) for b in range(NZ)
    ]


def position():
    me = lax.axis_index("tp")
    x, z = me // NZ, me % NZ
    even = lax.axis_index("ctx") % 2 == 0
    return even, jnp.where(even, x, z), jnp.where(even, z, x)


def send_core(value):
    return lax.ppermute(value, "ctx", [(i, i ^ 1) for i in range(NY * 2)])


def order_kernel(x_ref, dep_ref, out_ref):
    pass


def after(value, dep):
    return pl.pallas_call(
        order_kernel,
        in_specs=[pl.BlockSpec(memory_space=pl.ANY)] * 2,
        out_specs=pl.BlockSpec(memory_space=pl.ANY),
        out_shape=jax.ShapeDtypeStruct(value.shape, value.dtype),
        input_output_aliases={0: 0},
    )(value, dep)


def gather_features(block):
    up, down, far = [send(block, step, 0) for step in STEPS[1:]]
    near, rest = jnp.stack([block, up]), jnp.stack([down, far])
    near = after(near, rest)
    rest = after(rest, near)
    near_up, rest_down = send(near, 0, 1), send(rest, 0, -1)
    near_down, rest_up = send(near, 0, -1), send(rest, 0, 1)
    near_far, rest_far = send(near_up, 0, 1), send(rest_down, 0, -1)
    return [near, rest, near_up, rest_up, near_down, rest_down, near_far, rest_far]


def block_ids():
    even, first, second = position()
    ids = []
    for b in STEPS:
        for a in STEPS:
            i, j = (first - a) % NX, (second - b) % NZ
            ids.append(jnp.where(even, i * NZ + j, j * NZ + i))
    return jnp.stack(ids).astype(jnp.int32)


def sibling_ids():
    me = lax.axis_index("ctx")
    return jnp.stack([((me >> 1) ^ 1) * 2, ((me >> 2) ^ 1) * 4]).astype(jnp.int32)


def project_kernel(ids, sibs, *refs):
    parts = refs[:8]
    w_ref, full_ref, q_ref, kv_ref, first_ref, others_ref, second_ref, last_ref = refs[8:]
    step = pl.program_id(0)
    for i in range(16):
        start = pl.multiple_of(ids[i] * 128, 128)
        full_ref[:, pl.ds(start, 128)] = parts[i // 2][i % 2]
    out = mm(full_ref[...], w_ref[...]).astype(BF)
    q_ref[...] = out[:, :DH]
    kv = out[:, DH:]
    kv_ref[...] = kv
    rows = kv.shape[0]
    for l, ref in enumerate((first_ref, second_ref, last_ref)):
        width = RATIO * 2**l
        count = rows // width
        window = lax.broadcasted_iota(jnp.int32, (count, rows), 0)
        row = lax.broadcasted_iota(jnp.int32, (count, rows), 1)
        inside = jnp.where((row >= window * width) & (row < (window + 1) * width), 1.0, 0.0)
        means = mm(inside.astype(BF), kv) * (1.0 / width)
        if l == 0:
            ref[...] = means.astype(BF)
        else:
            ref[pl.ds(pl.multiple_of(step * count, count), count), :] = means

    @pl.when(step == pl.num_programs(0) - 1)
    def _():
        second = second_ref[...].astype(BF)
        last = last_ref[...].astype(BF)
        for d in range(NY * 2):
            others_ref[d] = second
        for d in range(4):
            others_ref[pl.ds(sibs[1] + d, 1), : last.shape[0]] = last[None]


def project(ids, sibs, parts, weight):
    n = parts[0].shape[1]
    feats = 16 * 128
    rows = 512
    row_map = lambda i, ids, sibs: (i, 0)
    coarse = n // RATIO
    return pl.pallas_call(
        project_kernel,
        grid_spec=pltpu.PrefetchScalarGridSpec(
            num_scalar_prefetch=2,
            grid=(n // rows,),
            in_specs=[pl.BlockSpec((2, rows, 128), lambda i, ids, sibs: (0, i, 0))] * 8
            + [pl.BlockSpec(weight.shape, lambda i, ids, sibs: (0, 0))],
            out_specs=[
                pl.BlockSpec((rows, feats), row_map),
                pl.BlockSpec((rows, DH), row_map),
                pl.BlockSpec((rows, 2 * DH), row_map),
                pl.BlockSpec((rows // RATIO, 2 * DH), row_map),
                pl.BlockSpec((NY * 2, coarse // 2, 2 * DH), lambda i, ids, sibs: (0, 0, 0)),
            ],
            scratch_shapes=[
                pltpu.VMEM((coarse // 2, 2 * DH), F32),
                pltpu.VMEM((coarse // 4, 2 * DH), F32),
            ],
        ),
        out_shape=[
            jax.ShapeDtypeStruct((n, feats), BF),
            jax.ShapeDtypeStruct((n, DH), BF),
            jax.ShapeDtypeStruct((n, 2 * DH), BF),
            jax.ShapeDtypeStruct((coarse, 2 * DH), BF),
            jax.ShapeDtypeStruct((NY * 2, coarse // 2, 2 * DH), BF),
        ],
        compiler_params=pltpu.CompilerParams(vmem_limit_bytes=60 * 2**20),
        cost_estimate=pl.CostEstimate(
            flops=6 * n * feats * DH, bytes_accessed=4 * n * feats, transcendentals=0
        ),
    )(ids, sibs, *parts, weight)


def add_bias(scores, own, coarse):
    out = [scores[:own]]
    for l in range((scores.shape[0] - own) // coarse):
        low = own + l * coarse
        out.append(scores[low : low + coarse] + math.log(RATIO * 2**l) * LOG2E)
    return jnp.concatenate(out, axis=0)


def attention_kernel(
    own, coarse, sibs, q_ref, kv_ref, first_ref, others_ref, cot_ref, wo_ref,
    att_ref, dq_ref, dkv_ref, dfirst_ref, dothers_ref, k_ref, v_ref, kt_ref, vt_ref, acc_ref,
):
    step = pl.program_id(0)

    @pl.when(step == 0)
    def _():
        half, quarter = coarse // 2, coarse // 4
        pieces = [(0, kv_ref[...]), (own, first_ref[...])]
        for d in range(2):
            pieces.append((own + coarse + d * half, others_ref[pl.ds(sibs[0] + d, 1)][0]))
        for d in range(4):
            rows = others_ref[pl.ds(sibs[1] + d, 1)][0, :quarter]
            pieces.append((own + 2 * coarse + d * quarter, rows))
        for low, rows in pieces:
            k_ref[low : low + rows.shape[0]] = rows[:, :DH]
            v_ref[low : low + rows.shape[0]] = rows[:, DH:]
        kt_ref[...] = k_ref[...].T
        vt_ref[...] = v_ref[...].T
        acc_ref[...] = jnp.zeros_like(acc_ref)

    q = q_ref[...]
    d_att = mm(cot_ref[...], wo_ref[...], NT).astype(BF)
    scores = mm(k_ref[...], q, NT) * (DH**-0.5 * LOG2E)
    scores = add_bias(scores, own, coarse)
    d_probs = mm(v_ref[...], d_att, NT)
    peak = jnp.max(scores, axis=0, keepdims=True)
    expo = jnp.exp2(scores - peak)
    probs = expo * (1.0 / jnp.sum(expo, axis=0, keepdims=True))
    delta = jnp.sum(probs * d_probs, axis=0, keepdims=True)
    d_scores = (DH**-0.5 * probs * (d_probs - delta)).astype(BF)
    probs = probs.astype(BF)
    att_ref[...] = mm(vt_ref[...], probs).astype(BF)
    dq_ref[...] = mm(kt_ref[...], d_scores).T.astype(BF)
    acc_ref[:, :DH] += mm(d_scores, q)
    acc_ref[:, DH:] += mm(probs, d_att)

    @pl.when(step == pl.num_programs(0) - 1)
    def _():
        half, quarter = coarse // 2, coarse // 4
        dkv_ref[...] = acc_ref[:own]
        dfirst_ref[...] = acc_ref[own : own + coarse]
        dothers_ref[...] = jnp.zeros_like(dothers_ref)
        for d in range(2):
            low = own + coarse + d * half
            dothers_ref[pl.ds(sibs[0] + d, 1)] = acc_ref[low : low + half][None]
        for d in range(4):
            low = own + 2 * coarse + d * quarter
            dothers_ref[pl.ds(sibs[1] + d, 1), :quarter] = acc_ref[low : low + quarter][None]


def attention(sibs, queries, listed, first, others, cot, w_out):
    n, feats = cot.shape
    own, coarse = listed.shape[0], first.shape[0]
    m = own + 3 * coarse
    rows = 512
    whole = lambda i, sibs: (0, 0)
    blocks = lambda i, sibs: (0, 0, 0)
    return pl.pallas_call(
        functools.partial(attention_kernel, own, coarse),
        grid_spec=pltpu.PrefetchScalarGridSpec(
            num_scalar_prefetch=1,
            grid=(n // rows,),
            in_specs=[
                pl.BlockSpec((rows, DH), lambda i, sibs: (i, 0)),
                pl.BlockSpec(listed.shape, whole),
                pl.BlockSpec(first.shape, whole),
                pl.BlockSpec(others.shape, blocks),
                pl.BlockSpec((rows, feats), lambda i, sibs: (i, 0)),
                pl.BlockSpec((DH, feats), whole),
            ],
            out_specs=[
                pl.BlockSpec((DH, rows), lambda i, sibs: (0, i)),
                pl.BlockSpec((rows, DH), lambda i, sibs: (i, 0)),
                pl.BlockSpec(listed.shape, whole),
                pl.BlockSpec(first.shape, whole),
                pl.BlockSpec(others.shape, blocks),
            ],
            scratch_shapes=[
                pltpu.VMEM((m, DH), BF),
                pltpu.VMEM((m, DH), BF),
                pltpu.VMEM((DH, m), BF),
                pltpu.VMEM((DH, m), BF),
                pltpu.VMEM((m, 2 * DH), F32),
            ],
        ),
        out_shape=[
            jax.ShapeDtypeStruct((DH, n), BF),
            jax.ShapeDtypeStruct((n, DH), BF),
            jax.ShapeDtypeStruct(listed.shape, F32),
            jax.ShapeDtypeStruct(first.shape, F32),
            jax.ShapeDtypeStruct(others.shape, F32),
        ],
        compiler_params=pltpu.CompilerParams(vmem_limit_bytes=60 * 2**20),
        cost_estimate=pl.CostEstimate(
            flops=24 * n * m * DH, bytes_accessed=2 * n * feats, transcendentals=n * m
        ),
    )(sibs, queries, listed, first, others, cot, w_out)


def token_grad_kernel(ids, d_ref, *refs):
    weights, outs = refs[:NZ], refs[NZ:]
    d = jnp.concatenate([d_ref[i] for i in range(NX)], axis=1)
    w = jnp.concatenate(
        [jnp.concatenate([w_ref[i] for w_ref in weights], axis=0) for i in range(NX)], axis=1
    )
    out = mm(d, w, NT)
    for step, out_ref in enumerate(outs):
        out_ref[0] = out[:, step * DH : (step + 1) * DH]


def token_grad_parts(d_rows, weights):
    heads, rows, cols = d_rows.shape
    even, _, second = position()
    ids = []
    for i in range(NX):
        for step in range(NZ):
            j = (second + step) % NZ
            ids.append(jnp.where(even, i * NZ + j, j * NZ + i))
    ids = jnp.stack(ids).astype(jnp.int32)

    def column(step):
        return pl.BlockSpec((heads, DH, cols), lambda i, ids: (0, ids[i * NZ + step], 0))

    return pl.pallas_call(
        token_grad_kernel,
        grid_spec=pltpu.PrefetchScalarGridSpec(
            num_scalar_prefetch=1,
            grid=(NX,),
            in_specs=[pl.BlockSpec((heads, rows, cols), lambda i, ids: (0, 0, 0))]
            + [column(step) for step in range(NZ)],
            out_specs=[pl.BlockSpec((1, rows, DH), lambda i, ids: (i, 0, 0))] * NZ,
        ),
        out_shape=[jax.ShapeDtypeStruct((NX, rows, DH), F32)] * NZ,
        compiler_params=pltpu.CompilerParams(vmem_limit_bytes=60 * 2**20),
        cost_estimate=pl.CostEstimate(
            flops=2 * heads * rows * cols * 2048,
            bytes_accessed=2 * heads * cols * 2048 + 8192 * rows,
            transcendentals=0,
        ),
    )(ids, d_rows, weights, weights, weights, weights)


def out_grad_kernel(x_ref, a_ref, out_ref):
    grads = mm(a_ref[...], x_ref[...]).T
    for i in range(out_ref.shape[0]):
        out_ref[i, 0] = grads[i * out_ref.shape[2] : (i + 1) * out_ref.shape[2]]


def out_grads(cot, attended_t):
    n, f = cot.shape
    chunk = f // (2 * NY)
    return pl.pallas_call(
        out_grad_kernel,
        grid=(NY,),
        in_specs=[
            pl.BlockSpec((n, 2 * chunk), lambda i: (0, i)),
            pl.BlockSpec((DH, n), lambda i: (0, 0)),
        ],
        out_specs=pl.BlockSpec((2, 1, chunk, DH), lambda i: (i, 3, 0, 0)),
        out_shape=jax.ShapeDtypeStruct((2 * NY, 4, chunk, DH), F32),
        compiler_params=pltpu.CompilerParams(vmem_limit_bytes=60 * 2**20),
        cost_estimate=pl.CostEstimate(
            flops=2 * n * f * DH, bytes_accessed=2 * n * f, transcendentals=0
        ),
    )(cot, attended_t)


def weight_grad_kernel(
    sibs, x_ref, dq_ref, own_ref, first_ref, others_ref, alias_ref, out_ref, d_ref, dt_ref
):
    @pl.when(pl.program_id(0) == 0)
    def _():
        coarse, cols = first_ref.shape
        half, quarter = coarse // 2, coarse // 4
        second = sum(others_ref[pl.ds(sibs[0] + d, 1)][0] for d in range(2))
        last = sum(others_ref[pl.ds(sibs[1] + d, 1)][0, :quarter] for d in range(4))
        total = own_ref[...]
        for l, grads in enumerate((first_ref[...], second, last)):
            width = RATIO * 2**l
            spread = jnp.broadcast_to(
                (grads * (1.0 / width))[:, None, :], (grads.shape[0], width, cols)
            )
            total = total + spread.reshape(total.shape)
        d_ref[:, :DH] = dq_ref[...]
        d_ref[:, DH:] = total.astype(BF)
        dt_ref[...] = d_ref[...].T

    grads = mm(dt_ref[...], x_ref[...]).T
    chunk = out_ref.shape[2]
    for i in range(out_ref.shape[0]):
        for j in range(3):
            out_ref[i, j] = grads[i * chunk : (i + 1) * chunk, j * DH : (j + 1) * DH]


def weight_grads(sibs, feats, d_queries, own, first, others, out):
    n, f = feats.shape
    chunk = f // (2 * NY)
    whole = lambda i, sibs: (0, 0)
    return pl.pallas_call(
        weight_grad_kernel,
        grid_spec=pltpu.PrefetchScalarGridSpec(
            num_scalar_prefetch=1,
            grid=(NY,),
            in_specs=[
                pl.BlockSpec((n, 2 * chunk), lambda i, sibs: (0, i)),
                pl.BlockSpec(d_queries.shape, whole),
                pl.BlockSpec(own.shape, whole),
                pl.BlockSpec(first.shape, whole),
                pl.BlockSpec(others.shape, lambda i, sibs: (0, 0, 0)),
                pl.BlockSpec(memory_space=pl.ANY),
            ],
            out_specs=[
                pl.BlockSpec((2, 3, chunk, DH), lambda i, sibs: (i, 0, 0, 0)),
                pl.BlockSpec((n, 3 * DH), whole),
            ],
            scratch_shapes=[pltpu.VMEM((3 * DH, n), BF)],
        ),
        out_shape=[
            jax.ShapeDtypeStruct(out.shape, F32),
            jax.ShapeDtypeStruct((n, 3 * DH), BF),
        ],
        input_output_aliases={6: 0},
        compiler_params=pltpu.CompilerParams(vmem_limit_bytes=60 * 2**20),
        cost_estimate=pl.CostEstimate(
            flops=6 * n * f * DH, bytes_accessed=2 * n * f + 12 * f * DH, transcendentals=0
        ),
    )(sibs, feats, d_queries, own, first, others, out)


def body(tokens, cotangent, w_query, w_key, w_value, w_out):
    own = tokens.shape[0]
    ids, sibs, lines = block_ids(), sibling_ids(), first_lines()
    weights = jnp.concatenate([w_query, w_key, w_value], axis=1)
    tok_parts = gather_features(tokens)
    cot = lax.all_gather(after(cotangent, tok_parts[1]), "tp", axis=1, tiled=True)
    feats, queries, keys_values, first, others = project(ids, sibs, tok_parts, weights)
    others = lax.all_to_all(others, "ctx", 0, 0)
    first = send_core(first)
    weight_heads = lax.all_gather(
        after(weights, queries), ("ctx", "tp"), axis_index_groups=lines
    )
    attended_t, d_queries, d_own, d_first, d_others = attention(
        sibs, queries, keys_values, first, others, cot, w_out
    )
    grads = out_grads(cot, attended_t)
    d_others = lax.all_to_all(d_others, "ctx", 0, 0)
    d_first = send_core(d_first)
    grads, d_all = weight_grads(sibs, feats, d_queries, d_own, d_first, d_others, grads)
    grads = lax.psum_scatter(after(grads, weight_heads), "ctx", scatter_dimension=0)
    d_rows = d_all.reshape(NX, own // NX, 3 * DH)
    d_rows = lax.all_to_all(d_rows, ("ctx", "tp"), 0, 0, axis_index_groups=lines)
    parts = token_grad_parts(d_rows, weight_heads)
    grads = lax.all_gather(after(grads, parts[0]), "ctx")
    query_grad, key_grad, value_grad, out_grad = [
        grads[:, i].reshape(-1, DH) for i in range(4)
    ]
    out_grad = out_grad.T
    total = parts[0]
    for step in range(1, NZ):
        total = total + send(parts[step], 0, step)
    total = after(total.astype(BF), grads)
    token_grad = lax.all_to_all(total, ("ctx", "tp"), 0, 0, axis_index_groups=lines)
    token_grad = token_grad.reshape(own, DH)
    return (token_grad, query_grad, key_grad, value_grad, out_grad)


def solution(mesh):
    return jax.shard_map(
        body,
        mesh=mesh,
        in_specs=(
            P("ctx", "tp"),
            P("ctx", "tp"),
            P(None, "tp"),
            P(None, "tp"),
            P(None, "tp"),
            P("tp", None),
        ),
        out_specs=(P("ctx", "tp"), P(None, "tp"), P(None, "tp"), P(None, "tp"), P("tp", None)),
        check_vma=False,
    )
```

```python
import functools
import math

import jax
import jax.numpy as jnp
from jax import lax
from jax.experimental import pallas as pl
from jax.experimental.pallas import tpu as pltpu
from jax.sharding import PartitionSpec as P

DH = 128
RATIO = 16
NX = 4
NZ = 4
NY = 4
BF = jnp.bfloat16
F32 = jnp.float32
STEPS = (0, 1, -1, 2)
LOG2E = 1.0 / math.log(2.0)
NT = (((1,), (1,)), ((), ()))
NN = (((1,), (0,)), ((), ()))


def mm(a, b, dims=NN):
    return lax.dot_general(a, b, dims, preferred_element_type=F32)


def place(ctx, first, second):
    x, z = (first, second) if ctx % 2 == 0 else (second, first)
    return ctx * NX * NZ + x * NZ + z


def send(value, first, second):
    pairs = [
        (place(ctx, a, b), place(ctx, (a + first) % NX, (b + second) % NZ))
        for ctx in range(NY * 2)
        for a in range(NX)
        for b in range(NZ)
    ]
    return lax.ppermute(value, ("ctx", "tp"), pairs)


def first_lines():
    return [
        [place(ctx, a, b) for a in range(NX)] for ctx in range(NY * 2) for b in range(NZ)
    ]


def position():
    me = lax.axis_index("tp")
    x, z = me // NZ, me % NZ
    even = lax.axis_index("ctx") % 2 == 0
    return even, jnp.where(even, x, z), jnp.where(even, z, x)


def send_core(value):
    return lax.ppermute(value, "ctx", [(i, i ^ 1) for i in range(NY * 2)])


def order_kernel(x_ref, dep_ref, out_ref):
    pass


def after(value, dep):
    return pl.pallas_call(
        order_kernel,
        in_specs=[pl.BlockSpec(memory_space=pl.ANY)] * 2,
        out_specs=pl.BlockSpec(memory_space=pl.ANY),
        out_shape=jax.ShapeDtypeStruct(value.shape, value.dtype),
        input_output_aliases={0: 0},
    )(value, dep)


def gather_features(block):
    up, down, far = [send(block, step, 0) for step in STEPS[1:]]
    near, rest = jnp.stack([block, up]), jnp.stack([down, far])
    near = after(near, rest)
    rest = after(rest, near)
    near_up, rest_down = send(near, 0, 1), send(rest, 0, -1)
    near_down, rest_up = send(near, 0, -1), send(rest, 0, 1)
    near_far, rest_far = send(near_up, 0, 1), send(rest_down, 0, -1)
    return [near, rest, near_up, rest_up, near_down, rest_down, near_far, rest_far]


def block_ids():
    even, first, second = position()
    ids = []
    for b in STEPS:
        for a in STEPS:
            i, j = (first - a) % NX, (second - b) % NZ
            ids.append(jnp.where(even, i * NZ + j, j * NZ + i))
    return jnp.stack(ids).astype(jnp.int32)


def sibling_ids():
    me = lax.axis_index("ctx")
    return jnp.stack([((me >> 1) ^ 1) * 2, ((me >> 2) ^ 1) * 4]).astype(jnp.int32)


def project_kernel(ids, sibs, *refs):
    parts = refs[:8]
    w_ref, full_ref, q_ref, kv_ref, first_ref, others_ref, second_ref, last_ref = refs[8:]
    step = pl.program_id(0)
    for i in range(16):
        start = pl.multiple_of(ids[i] * 128, 128)
        full_ref[:, pl.ds(start, 128)] = parts[i // 2][i % 2]
    out = mm(full_ref[...], w_ref[...]).astype(BF)
    q_ref[...] = out[:, :DH]
    kv = out[:, DH:]
    kv_ref[...] = kv
    rows = kv.shape[0]
    for l, ref in enumerate((first_ref, second_ref, last_ref)):
        width = RATIO * 2**l
        count = rows // width
        window = lax.broadcasted_iota(jnp.int32, (count, rows), 0)
        row = lax.broadcasted_iota(jnp.int32, (count, rows), 1)
        inside = jnp.where((row >= window * width) & (row < (window + 1) * width), 1.0, 0.0)
        means = mm(inside.astype(BF), kv) * (1.0 / width)
        if l == 0:
            ref[...] = means.astype(BF)
        else:
            ref[pl.ds(pl.multiple_of(step * count, count), count), :] = means

    @pl.when(step == pl.num_programs(0) - 1)
    def _():
        second = second_ref[...].astype(BF)
        last = last_ref[...].astype(BF)
        for d in range(NY * 2):
            others_ref[d] = second
        for d in range(4):
            others_ref[pl.ds(sibs[1] + d, 1), : last.shape[0]] = last[None]


def project(ids, sibs, parts, weight):
    n = parts[0].shape[1]
    feats = 16 * 128
    rows = 512
    row_map = lambda i, ids, sibs: (i, 0)
    coarse = n // RATIO
    return pl.pallas_call(
        project_kernel,
        grid_spec=pltpu.PrefetchScalarGridSpec(
            num_scalar_prefetch=2,
            grid=(n // rows,),
            in_specs=[pl.BlockSpec((2, rows, 128), lambda i, ids, sibs: (0, i, 0))] * 8
            + [pl.BlockSpec(weight.shape, lambda i, ids, sibs: (0, 0))],
            out_specs=[
                pl.BlockSpec((rows, feats), row_map),
                pl.BlockSpec((rows, DH), row_map),
                pl.BlockSpec((rows, 2 * DH), row_map),
                pl.BlockSpec((rows // RATIO, 2 * DH), row_map),
                pl.BlockSpec((NY * 2, coarse // 2, 2 * DH), lambda i, ids, sibs: (0, 0, 0)),
            ],
            scratch_shapes=[
                pltpu.VMEM((coarse // 2, 2 * DH), F32),
                pltpu.VMEM((coarse // 4, 2 * DH), F32),
            ],
        ),
        out_shape=[
            jax.ShapeDtypeStruct((n, feats), BF),
            jax.ShapeDtypeStruct((n, DH), BF),
            jax.ShapeDtypeStruct((n, 2 * DH), BF),
            jax.ShapeDtypeStruct((coarse, 2 * DH), BF),
            jax.ShapeDtypeStruct((NY * 2, coarse // 2, 2 * DH), BF),
        ],
        compiler_params=pltpu.CompilerParams(vmem_limit_bytes=60 * 2**20),
        cost_estimate=pl.CostEstimate(
            flops=6 * n * feats * DH, bytes_accessed=4 * n * feats, transcendentals=0
        ),
    )(ids, sibs, *parts, weight)


def add_bias(scores, own, coarse):
    out = [scores[:own]]
    for l in range((scores.shape[0] - own) // coarse):
        low = own + l * coarse
        out.append(scores[low : low + coarse] + math.log(RATIO * 2**l) * LOG2E)
    return jnp.concatenate(out, axis=0)


def attention_kernel(
    own, coarse, sibs, q_ref, kv_ref, first_ref, others_ref, cot_ref, wo_ref,
    att_ref, dq_ref, dkv_ref, dfirst_ref, dothers_ref, k_ref, v_ref, kt_ref, vt_ref, acc_ref,
):
    step = pl.program_id(0)

    @pl.when(step == 0)
    def _():
        half, quarter = coarse // 2, coarse // 4
        pieces = [(0, kv_ref[...]), (own, first_ref[...])]
        for d in range(2):
            pieces.append((own + coarse + d * half, others_ref[pl.ds(sibs[0] + d, 1)][0]))
        for d in range(4):
            rows = others_ref[pl.ds(sibs[1] + d, 1)][0, :quarter]
            pieces.append((own + 2 * coarse + d * quarter, rows))
        for low, rows in pieces:
            k_ref[low : low + rows.shape[0]] = rows[:, :DH]
            v_ref[low : low + rows.shape[0]] = rows[:, DH:]
        kt_ref[...] = k_ref[...].T
        vt_ref[...] = v_ref[...].T
        acc_ref[...] = jnp.zeros_like(acc_ref)

    q = q_ref[...]
    d_att = mm(cot_ref[...], wo_ref[...], NT).astype(BF)
    scores = mm(k_ref[...], q, NT) * (DH**-0.5 * LOG2E)
    scores = add_bias(scores, own, coarse)
    d_probs = mm(v_ref[...], d_att, NT)
    peak = jnp.max(scores, axis=0, keepdims=True)
    expo = jnp.exp2(scores - peak)
    probs = expo * (1.0 / jnp.sum(expo, axis=0, keepdims=True))
    delta = jnp.sum(probs * d_probs, axis=0, keepdims=True)
    d_scores = (DH**-0.5 * probs * (d_probs - delta)).astype(BF)
    probs = probs.astype(BF)
    att_ref[...] = mm(vt_ref[...], probs).astype(BF)
    dq_ref[...] = mm(kt_ref[...], d_scores).T.astype(BF)
    acc_ref[:, :DH] += mm(d_scores, q)
    acc_ref[:, DH:] += mm(probs, d_att)

    @pl.when(step == pl.num_programs(0) - 1)
    def _():
        half, quarter = coarse // 2, coarse // 4
        dkv_ref[...] = acc_ref[:own]
        dfirst_ref[...] = acc_ref[own : own + coarse]
        dothers_ref[...] = jnp.zeros_like(dothers_ref)
        for d in range(2):
            low = own + coarse + d * half
            dothers_ref[pl.ds(sibs[0] + d, 1)] = acc_ref[low : low + half][None]
        for d in range(4):
            low = own + 2 * coarse + d * quarter
            dothers_ref[pl.ds(sibs[1] + d, 1), :quarter] = acc_ref[low : low + quarter][None]


def attention(sibs, queries, listed, first, others, cot, w_out):
    n, feats = cot.shape
    own, coarse = listed.shape[0], first.shape[0]
    m = own + 3 * coarse
    rows = 512
    whole = lambda i, sibs: (0, 0)
    blocks = lambda i, sibs: (0, 0, 0)
    return pl.pallas_call(
        functools.partial(attention_kernel, own, coarse),
        grid_spec=pltpu.PrefetchScalarGridSpec(
            num_scalar_prefetch=1,
            grid=(n // rows,),
            in_specs=[
                pl.BlockSpec((rows, DH), lambda i, sibs: (i, 0)),
                pl.BlockSpec(listed.shape, whole),
                pl.BlockSpec(first.shape, whole),
                pl.BlockSpec(others.shape, blocks),
                pl.BlockSpec((rows, feats), lambda i, sibs: (i, 0)),
                pl.BlockSpec((DH, feats), whole),
            ],
            out_specs=[
                pl.BlockSpec((DH, rows), lambda i, sibs: (0, i)),
                pl.BlockSpec((rows, DH), lambda i, sibs: (i, 0)),
                pl.BlockSpec(listed.shape, whole),
                pl.BlockSpec(first.shape, whole),
                pl.BlockSpec(others.shape, blocks),
            ],
            scratch_shapes=[
                pltpu.VMEM((m, DH), BF),
                pltpu.VMEM((m, DH), BF),
                pltpu.VMEM((DH, m), BF),
                pltpu.VMEM((DH, m), BF),
                pltpu.VMEM((m, 2 * DH), F32),
            ],
        ),
        out_shape=[
            jax.ShapeDtypeStruct((DH, n), BF),
            jax.ShapeDtypeStruct((n, DH), BF),
            jax.ShapeDtypeStruct(listed.shape, F32),
            jax.ShapeDtypeStruct(first.shape, F32),
            jax.ShapeDtypeStruct(others.shape, F32),
        ],
        compiler_params=pltpu.CompilerParams(vmem_limit_bytes=60 * 2**20),
        cost_estimate=pl.CostEstimate(
            flops=24 * n * m * DH, bytes_accessed=2 * n * feats, transcendentals=n * m
        ),
    )(sibs, queries, listed, first, others, cot, w_out)


def token_grad_kernel(ids, d_ref, *refs):
    weights, outs = refs[:NZ], refs[NZ:]
    d = jnp.concatenate([d_ref[i] for i in range(NX)], axis=1)
    w = jnp.concatenate(
        [jnp.concatenate([w_ref[i] for w_ref in weights], axis=0) for i in range(NX)], axis=1
    )
    out = mm(d, w, NT)
    for step, out_ref in enumerate(outs):
        out_ref[0] = out[:, step * DH : (step + 1) * DH]


def token_grad_parts(d_rows, weights):
    heads, rows, cols = d_rows.shape
    even, _, second = position()
    ids = []
    for i in range(NX):
        for step in range(NZ):
            j = (second + step) % NZ
            ids.append(jnp.where(even, i * NZ + j, j * NZ + i))
    ids = jnp.stack(ids).astype(jnp.int32)

    def column(step):
        return pl.BlockSpec((heads, DH, cols), lambda i, ids: (0, ids[i * NZ + step], 0))

    return pl.pallas_call(
        token_grad_kernel,
        grid_spec=pltpu.PrefetchScalarGridSpec(
            num_scalar_prefetch=1,
            grid=(NX,),
            in_specs=[pl.BlockSpec((heads, rows, cols), lambda i, ids: (0, 0, 0))]
            + [column(step) for step in range(NZ)],
            out_specs=[pl.BlockSpec((1, rows, DH), lambda i, ids: (i, 0, 0))] * NZ,
        ),
        out_shape=[jax.ShapeDtypeStruct((NX, rows, DH), F32)] * NZ,
        compiler_params=pltpu.CompilerParams(vmem_limit_bytes=60 * 2**20),
        cost_estimate=pl.CostEstimate(
            flops=2 * heads * rows * cols * 2048,
            bytes_accessed=2 * heads * cols * 2048 + 8192 * rows,
            transcendentals=0,
        ),
    )(ids, d_rows, weights, weights, weights, weights)


def out_grad_kernel(x_ref, a_ref, out_ref):
    grads = mm(a_ref[...], x_ref[...]).T
    for i in range(out_ref.shape[0]):
        out_ref[i, 0] = grads[i * out_ref.shape[2] : (i + 1) * out_ref.shape[2]]


def out_grads(cot, attended_t):
    n, f = cot.shape
    chunk = f // (2 * NY)
    return pl.pallas_call(
        out_grad_kernel,
        grid=(NY,),
        in_specs=[
            pl.BlockSpec((n, 2 * chunk), lambda i: (0, i)),
            pl.BlockSpec((DH, n), lambda i: (0, 0)),
        ],
        out_specs=pl.BlockSpec((2, 1, chunk, DH), lambda i: (i, 3, 0, 0)),
        out_shape=jax.ShapeDtypeStruct((2 * NY, 4, chunk, DH), F32),
        compiler_params=pltpu.CompilerParams(vmem_limit_bytes=60 * 2**20),
        cost_estimate=pl.CostEstimate(
            flops=2 * n * f * DH, bytes_accessed=2 * n * f, transcendentals=0
        ),
    )(cot, attended_t)


def weight_grad_kernel(
    sibs, x_ref, dq_ref, own_ref, first_ref, others_ref, alias_ref, out_ref, d_ref, dt_ref
):
    @pl.when(pl.program_id(0) == 0)
    def _():
        coarse, cols = first_ref.shape
        half, quarter = coarse // 2, coarse // 4
        second = sum(others_ref[pl.ds(sibs[0] + d, 1)][0] for d in range(2))
        last = sum(others_ref[pl.ds(sibs[1] + d, 1)][0, :quarter] for d in range(4))
        total = own_ref[...]
        for l, grads in enumerate((first_ref[...], second, last)):
            width = RATIO * 2**l
            spread = jnp.broadcast_to(
                (grads * (1.0 / width))[:, None, :], (grads.shape[0], width, cols)
            )
            total = total + spread.reshape(total.shape)
        d_ref[:, :DH] = dq_ref[...]
        d_ref[:, DH:] = total.astype(BF)
        dt_ref[...] = d_ref[...].T

    grads = mm(dt_ref[...], x_ref[...]).T
    chunk = out_ref.shape[2]
    for i in range(out_ref.shape[0]):
        for j in range(3):
            out_ref[i, j] = grads[i * chunk : (i + 1) * chunk, j * DH : (j + 1) * DH]


def weight_grads(sibs, feats, d_queries, own, first, others, out):
    n, f = feats.shape
    chunk = f // (2 * NY)
    whole = lambda i, sibs: (0, 0)
    return pl.pallas_call(
        weight_grad_kernel,
        grid_spec=pltpu.PrefetchScalarGridSpec(
            num_scalar_prefetch=1,
            grid=(NY,),
            in_specs=[
                pl.BlockSpec((n, 2 * chunk), lambda i, sibs: (0, i)),
                pl.BlockSpec(d_queries.shape, whole),
                pl.BlockSpec(own.shape, whole),
                pl.BlockSpec(first.shape, whole),
                pl.BlockSpec(others.shape, lambda i, sibs: (0, 0, 0)),
                pl.BlockSpec(memory_space=pl.ANY),
            ],
            out_specs=[
                pl.BlockSpec((2, 3, chunk, DH), lambda i, sibs: (i, 0, 0, 0)),
                pl.BlockSpec((n, 3 * DH), whole),
            ],
            scratch_shapes=[pltpu.VMEM((3 * DH, n), BF)],
        ),
        out_shape=[
            jax.ShapeDtypeStruct(out.shape, F32),
            jax.ShapeDtypeStruct((n, 3 * DH), BF),
        ],
        input_output_aliases={6: 0},
        compiler_params=pltpu.CompilerParams(vmem_limit_bytes=60 * 2**20),
        cost_estimate=pl.CostEstimate(
            flops=6 * n * f * DH, bytes_accessed=2 * n * f + 12 * f * DH, transcendentals=0
        ),
    )(sibs, feats, d_queries, own, first, others, out)


def body(tokens, cotangent, w_query, w_key, w_value, w_out):
    own = tokens.shape[0]
    ids, sibs, lines = block_ids(), sibling_ids(), first_lines()
    weights = jnp.concatenate([w_query, w_key, w_value], axis=1)
    tok_parts = gather_features(tokens)
    ordered = cotangent + tok_parts[1][0, 0, 0] * 0
    cot = lax.all_gather(ordered, "tp", axis=1, tiled=True)
    feats, queries, keys_values, first, others = project(ids, sibs, tok_parts, weights)
    others = lax.all_to_all(others, "ctx", 0, 0)
    first = send_core(first)
    weight_heads = lax.all_gather(
        after(weights, queries), ("ctx", "tp"), axis_index_groups=lines
    )
    attended_t, d_queries, d_own, d_first, d_others = attention(
        sibs, queries, keys_values, first, others, cot, w_out
    )
    grads = out_grads(cot, attended_t)
    d_others = lax.all_to_all(d_others, "ctx", 0, 0)
    d_first = send_core(d_first)
    grads, d_all = weight_grads(sibs, feats, d_queries, d_own, d_first, d_others, grads)
    grads = lax.psum_scatter(after(grads, weight_heads), "ctx", scatter_dimension=0)
    d_rows = d_all.reshape(NX, own // NX, 3 * DH)
    d_rows = lax.all_to_all(d_rows, ("ctx", "tp"), 0, 0, axis_index_groups=lines)
    parts = token_grad_parts(d_rows, weight_heads)
    grads = lax.all_gather(after(grads, parts[0]), "ctx")
    query_grad, key_grad, value_grad, out_grad = [
        grads[:, i].reshape(-1, DH) for i in range(4)
    ]
    out_grad = out_grad.T
    total = parts[0]
    for step in range(1, NZ):
        total = total + send(parts[step], 0, step)
    total = after(total.astype(BF), grads)
    token_grad = lax.all_to_all(total, ("ctx", "tp"), 0, 0, axis_index_groups=lines)
    token_grad = token_grad.reshape(own, DH)
    return (token_grad, query_grad, key_grad, value_grad, out_grad)


def solution(mesh):
    return jax.shard_map(
        body,
        mesh=mesh,
        in_specs=(
            P("ctx", "tp"),
            P("ctx", "tp"),
            P(None, "tp"),
            P(None, "tp"),
            P(None, "tp"),
            P("tp", None),
        ),
        out_specs=(P("ctx", "tp"), P(None, "tp"), P(None, "tp"), P(None, "tp"), P("tp", None)),
        check_vma=False,
    )
```
